32 devices in a mesh: group: 2 (over x), seq: 4 (over y, core), tp: 4 (over z).
Axes of the slice: x: 2, y: 2, z: 4, core: 2. Of those that a mesh axis runs over, the one named last changes fastest.
Arguments:
- queries: bfloat16 [4096, 4096], P(('group', 'seq'), 'tp'), parts along dimension 0, may hold values from -32 to 32
- key_value: bfloat16 [4096, 2, 2048], P(('group', 'seq'), None, 'tp'), parts along dimension 0, may hold values from -32 to 32
- window_cache: bfloat16 [2048, 2, 2048], P('group', None, 'tp'), parts along dimension 0, may hold values from -5 to 5
- span_start: int32 [2], P('group'), parts along dimension 0, may hold values from 1024 to 30720
- hidden: bfloat16 [4096, 21504], P(('group', 'seq'), 'tp'), parts along dimension 0, may hold values from -6 to 6
- down_codes: int32 [21504, 2688], P('tp', 'seq'), may hold values from 0 to 15
- down_scales: int32 [168, 2688], P('tp', 'seq'), may hold values from 1 to 15
- out_weight: bfloat16 [4096, 2688], P('tp', 'seq'), may hold values from -0.375 to 0.375
Outputs:
- layer_update: bfloat16 [4096, 2688], P(('group', 'seq', 'tp')), parts along dimension 0
The draws below stay inside these ranges and needn't reach their ends.
There are 2 independent parts, one for each index of `group`. The reference program is written for one: setup_inputs(seed, part) draws one part's arguments, and reference() takes and returns one part's arrays. A program takes and returns all parts, laid end to end along the dimension named above; an argument that names none is the same for every part. Nothing has to cross between parts.
All inputs are finite; a program needn't handle non-finite values.
Results may differ from the reference program's by a relative error of at most 0.02.
Values may be sent and summed in bfloat16 or wider, within the bound.
A program may use at most 192 MiB of HBM per device.

```python
import jax
import jax.numpy as jnp
import numpy as np
from jax import lax

FF = 21504
HEADS = 32
KV_HEADS = 16
HD = 128
WINDOW = 1024
DW = 2688
GROUP = 128
TOKENS = 2048


def joint_draw(key):
    base = jax.random.fold_in(key, 1009)
    keys_split = jax.random.split(base, 2)
    wide_query = HEADS * HD
    wide_pair = KV_HEADS * HD
    query_rows = jax.random.truncated_normal(keys_split[0], -4.0, 4.0, (TOKENS, wide_query), jnp.float32)
    pair_rows = jax.random.truncated_normal(keys_split[1], -4.0, 4.0, (TOKENS, 2, wide_pair), jnp.float32)
    return (query_rows, pair_rows)


def draw_queries(key, part):
    return joint_draw(key)[0].astype(jnp.bfloat16)


def draw_key_value(key, part):
    return joint_draw(key)[1].astype(jnp.bfloat16)


def plant(drawn, rng, smallest, top_value):
    place = [jax.random.randint(jax.random.fold_in(rng, axis), (), 0, length) for axis, length in enumerate(drawn.shape)]
    longest = drawn.shape.index(max(drawn.shape))
    next_to = place[:longest] + [(place[longest] + 1) % drawn.shape[longest]] + place[longest + 1:]
    return drawn.at[tuple(place)].set(smallest).at[tuple(next_to)].set(top_value)


def level_of(key, dims, cuts, least, largest):
    loudness = 1.0
    for position, blocks in cuts:
        draws = jax.random.uniform(jax.random.fold_in(jax.random.fold_in(key, 6), position), (blocks,), jnp.float32, least / len(cuts), largest / len(cuts))
        loudness = loudness * jnp.repeat(jnp.exp(draws), dims[position] // blocks).reshape((-1,) + (1,) * (len(dims) - 1 - position))
    return loudness


def centred(stream_key, dims, spread, limit, cuts=(), held_as=jnp.bfloat16):
    values = jax.random.normal(stream_key, dims, jnp.float32) * spread
    if len(cuts) > 0:
        values = level_of(stream_key, dims, cuts, -0.22, 0.18) * values
    return jnp.clip(values, min=-limit, max=limit).astype(held_as)


def setup_inputs(seed: int = 0, part: int = 0) -> dict:
    streams_of = jax.random.split(jax.random.key(seed), 9)
    own_keys = jax.random.split(jax.random.fold_in(streams_of[8], part), 9)
    return {
        "queries": draw_queries(jax.random.fold_in(jax.random.fold_in(streams_of[8], part), 71), part),
        "key_value": draw_key_value(jax.random.fold_in(jax.random.fold_in(streams_of[8], part), 71), part),
        "window_cache": centred(own_keys[2], (WINDOW, 2, KV_HEADS * HD), 1.0, 5.0, ((2, 4),)),
        "span_start": jax.random.randint(own_keys[3], (1,), WINDOW, 32768 - TOKENS + 1).astype(jnp.int32),
        "hidden": centred(own_keys[4], (TOKENS, FF), 1.0, 6.0, ((0, 4), (1, 4))),
        "down_codes": plant(jax.random.randint(streams_of[5], (FF, DW), 0, 16), jax.random.fold_in(streams_of[5], 1), 0, 15).astype(jnp.int32),
        "down_scales": plant(jax.random.randint(streams_of[6], (FF // GROUP, DW), 1, 16), jax.random.fold_in(streams_of[6], 1), 1, 15).astype(jnp.int32),
        "out_weight": centred(streams_of[7], (HEADS * HD, DW), (HEADS * HD // 16) ** -0.5, 0.375, ((0, 4), (1, 4))),
    }


ROPE_BASE = 10000.0
SCORE_SCALE = 168.0 ** -0.5
CODE_STEP = 2.0 ** -14
INV_ROOT = 1344.0 ** -0.5


def bit_total(value_now):
    return (value_now & 1) + ((value_now >> 1) & 1) + ((value_now >> 2) & 1)


def build_tables():
    prime_order = 167
    residues = set((value_now * value_now) % prime_order for value_now in range(1, prime_order))
    legendre = [0] + [1 if value_now in residues else -1 for value_now in range(1, prime_order)]
    paley_table = np.eye(prime_order + 1)
    paley_table[0, 1:] += 1.0
    paley_table[1:, 0] -= 1.0
    for row_index in range(prime_order):
        for col_index in range(prime_order):
            paley_table[row_index + 1, col_index + 1] += legendre[(col_index - row_index) % prime_order]
    sylvester = np.array([[(-1.0) ** bit_total(left_bit & right_bit) for right_bit in range(8)] for left_bit in range(8)])
    return paley_table, sylvester


def rotary(values, cosine, sine_part):
    half_dim = values.shape[-1] // 2
    first_half = values[..., :half_dim]
    second_half = values[..., half_dim:]
    return jnp.concatenate([first_half * cosine - second_half * sine_part, second_half * cosine + first_half * sine_part], axis=-1)


def section_pairs(blocks_now, section_level):
    row_count, block_count, width_cols = blocks_now.shape
    paired = blocks_now.reshape(row_count, block_count >> (section_level + 1), 2, 1 << section_level, width_cols).astype(jnp.float32)
    upper_half = paired[:, :, 0]
    lower_half = paired[:, :, 1]
    mixed = jnp.stack([upper_half + lower_half, upper_half - lower_half], axis=2)
    return mixed.astype(jnp.bfloat16).reshape(row_count, block_count, width_cols)


def rotate_hidden(block_rows, paley_table, sylvester):
    row_count = block_rows.shape[0]
    parts_now = block_rows.astype(jnp.float32).reshape(row_count, 16, 8, 168)
    mixed = jnp.einsum("nbac,cd->nbad", parts_now, paley_table, precision=lax.Precision.HIGHEST)
    mixed = jnp.einsum("nbad,ae->nbed", mixed, sylvester, precision=lax.Precision.HIGHEST) * INV_ROOT
    blocks_now = mixed.reshape(row_count, 16, 1344).astype(jnp.bfloat16)
    for section_level in range(4):
        blocks_now = section_pairs(blocks_now, section_level)
    return blocks_now.reshape(row_count, 16 * 1344)


def reference(queries, key_value, window_cache, span_start, hidden, down_codes, down_scales, out_weight):
    first_pos = span_start[0]
    positions = (first_pos + jnp.arange(TOKENS, dtype=jnp.int32)).astype(jnp.float32)
    inv_freq = ROPE_BASE ** (-(2.0 * jnp.arange(HD // 2, dtype=jnp.float32)) / HD)
    angles = positions[:, None] * inv_freq[None, :]
    cosine = jnp.cos(angles)[:, None, :]
    sine_part = jnp.sin(angles)[:, None, :]
    query_rot = rotary(queries.astype(jnp.float32).reshape(TOKENS, HEADS, HD), cosine, sine_part).astype(jnp.bfloat16)
    key_rot = rotary(key_value[:, 0].astype(jnp.float32).reshape(TOKENS, KV_HEADS, HD), cosine, sine_part).astype(jnp.bfloat16)
    cycle_index = ((jnp.arange(WINDOW, dtype=jnp.int32) + first_pos % WINDOW) % WINDOW).astype(jnp.int32)
    ordered = jnp.take(window_cache, cycle_index, axis=0)
    all_keys = jnp.concatenate([ordered[:, 0].reshape(WINDOW, KV_HEADS, HD), key_rot], axis=0)
    all_values = jnp.concatenate([ordered[:, 1].reshape(WINDOW, KV_HEADS, HD), key_value[:, 1].reshape(TOKENS, KV_HEADS, HD)], axis=0)
    group_size = HEADS // KV_HEADS
    query_block = min(TOKENS, 512)

    def attend(block_first):
        grouped = lax.dynamic_slice_in_dim(query_rot, block_first, query_block, 0).astype(jnp.float32)
        grouped = grouped.reshape(query_block, KV_HEADS, group_size, HD)
        key_rows = lax.dynamic_slice_in_dim(all_keys, block_first, query_block + WINDOW, 0).astype(jnp.float32)
        value_rows = lax.dynamic_slice_in_dim(all_values, block_first, query_block + WINDOW, 0).astype(jnp.float32)
        scores = jnp.einsum("qkgd,skd->kgqs", grouped, key_rows) * SCORE_SCALE
        query_ids = jnp.arange(query_block)[:, None]
        key_ids = jnp.arange(query_block + WINDOW)[None, :]
        allowed = (key_ids > query_ids) & (key_ids <= query_ids + WINDOW)
        scores = jnp.where(allowed, scores, -jnp.inf)
        top_score = jnp.max(scores, axis=-1, keepdims=True)
        weights_soft = jnp.exp(scores - top_score)
        weights_soft = (weights_soft / jnp.sum(weights_soft, axis=-1, keepdims=True)).astype(jnp.bfloat16)
        attended = jnp.einsum("kgqs,skd->qkgd", weights_soft.astype(jnp.float32), value_rows)
        return attended.astype(jnp.bfloat16).reshape(query_block, HEADS * HD)

    block_starts = (jnp.arange(TOKENS // query_block, dtype=jnp.int32) * query_block).astype(jnp.int32)
    attn = lax.map(attend, block_starts).reshape(TOKENS, HEADS * HD)

    scale_rows = jnp.repeat(down_scales, GROUP, axis=0)
    down_weight = ((down_codes - 8) * scale_rows).astype(jnp.float32) * CODE_STEP
    weights_all = jnp.concatenate([down_weight.astype(jnp.bfloat16), out_weight], axis=0)
    paley_np, sylvester_np = build_tables()
    paley_table = jnp.asarray(paley_np, dtype=jnp.float32)
    sylvester = jnp.asarray(sylvester_np, dtype=jnp.float32)
    ffn_block = min(TOKENS, 1024)

    def project(block_first):
        block_rows = lax.dynamic_slice_in_dim(hidden, block_first, ffn_block, 0)
        side_rows = lax.dynamic_slice_in_dim(attn, block_first, ffn_block, 0)
        joined = jnp.concatenate([rotate_hidden(block_rows, paley_table, sylvester), side_rows], axis=1)
        return jnp.dot(joined, weights_all, preferred_element_type=jnp.float32).astype(jnp.bfloat16)

    ffn_starts = (jnp.arange(TOKENS // ffn_block, dtype=jnp.int32) * ffn_block).astype(jnp.int32)
    return lax.map(project, ffn_starts).reshape(TOKENS, DW)
```

```python
import jax
import jax.numpy as jnp
import numpy as np
from jax import lax
from jax.sharding import PartitionSpec as P

HD = 128
WINDOW = 1024
GROUP = 128
BLOCK = 1344
CHUNKS = 3


ROPE_BASE = 10000.0
SCORE_SCALE = 168.0 ** (-0.5)
CODE_STEP = 2.0 ** (-14)
INV_ROOT = 1344.0 ** (-0.5)


def shifted(value, axis, steps):
    count = lax.axis_size(axis)
    first, last = (max(0, -steps), min(count, count - steps))
    return lax.ppermute(value, axis, [(source, source + steps) for source in range(first, last)])


def swapped(x, axis, stride):
    return lax.ppermute(x, axis, [(i, i ^ 1 << stride) for i in range(lax.axis_size(axis))])


def block_mixer():
    order = 167
    residues = {value * value % order for value in range(1, order)}
    legendre = np.array([0] + [1 if value in residues else -1 for value in range(1, order)])
    paley = np.eye(order + 1)
    paley[0, 1:] += 1
    paley[1:, 0] -= 1
    places = np.arange(order)
    paley[1:, 1:] += legendre[(places[None, :] - places[:, None]) % order]
    pair = np.array([[1, 1], [1, -1]])
    return jnp.asarray(np.kron(np.kron(np.kron(pair, pair), pair), paley), jnp.bfloat16)


def gathered(piece):
    wide = lax.all_gather(piece, "group", axis=0, tiled=True)
    return lax.all_gather(wide, "seq", axis=1, tiled=True)


def rotary(values, cosine, sine_part):
    half_dim = values.shape[-1] // 2
    first_half = values[..., :half_dim]
    second_half = values[..., half_dim:]
    return jnp.concatenate(
        [
            first_half * cosine - second_half * sine_part,
            second_half * cosine + first_half * sine_part,
        ],
        axis=-1,
    )


def section_pairs(blocks_now, section_level):
    row_count, block_count, width_cols = blocks_now.shape
    paired = blocks_now.reshape(
        row_count, block_count >> section_level + 1, 2, 1 << section_level, width_cols
    ).astype(jnp.float32)
    upper_half = paired[:, :, 0]
    lower_half = paired[:, :, 1]
    mixed = jnp.stack([upper_half + lower_half, upper_half - lower_half], axis=2)
    return mixed.astype(jnp.bfloat16).reshape(row_count, block_count, width_cols)


def per_device(
    queries, key_value, window_cache, span_start, hidden, down_codes, down_scales, out_weight
):
    tok_rows = queries.shape[0]
    tp_count = lax.axis_size("tp")
    seq_index = lax.axis_index("seq")
    tp_index = lax.axis_index("tp")
    heads_dev = queries.shape[1] // HD
    kv_dev = key_value.shape[2] // HD
    group_size = heads_dev // kv_dev
    first_pos = span_start[0]
    positions = first_pos + seq_index * tok_rows + jnp.arange(tok_rows, dtype=jnp.int32)
    inv_freq = ROPE_BASE ** (-(2.0 * jnp.arange(HD // 2, dtype=jnp.float32)) / HD)
    angles = positions.astype(jnp.float32)[:, None] * inv_freq[None, :]
    cosine = jnp.cos(angles)[:, None, :]
    sine_part = jnp.sin(angles)[:, None, :]
    query_rot = rotary(
        queries.reshape(tok_rows, heads_dev, HD).astype(jnp.float32), cosine, sine_part
    ).astype(jnp.bfloat16)
    key_rot = rotary(
        key_value[:, 0].reshape(tok_rows, kv_dev, HD).astype(jnp.float32), cosine, sine_part
    ).astype(jnp.bfloat16)
    own_pairs = jnp.stack([key_rot.reshape(tok_rows, kv_dev * HD), key_value[:, 1]], axis=1)
    reach_blocks = WINDOW // tok_rows
    earlier = []
    moving = own_pairs
    for hop_count in range(reach_blocks):
        moving = shifted(moving, "seq", 1)
        earlier.insert(0, moving)
    halo_rows = jnp.concatenate(earlier, axis=0)
    doubled = jnp.concatenate([window_cache, window_cache], axis=0)
    ordered = lax.dynamic_slice_in_dim(doubled, first_pos % WINDOW, WINDOW, 0)
    padded_cache = jnp.concatenate([ordered, jnp.zeros_like(ordered)], axis=0)
    from_cache = lax.dynamic_slice_in_dim(
        padded_cache, jnp.minimum(seq_index * tok_rows, WINDOW), WINDOW, 0
    )
    halo_rows = halo_rows + from_cache
    all_rows = jnp.concatenate([halo_rows, own_pairs], axis=0)
    key_count = all_rows.shape[0]
    key_rows = all_rows[:, 0].reshape(key_count, kv_dev, HD)
    value_rows = all_rows[:, 1].reshape(key_count, kv_dev, HD)
    grouped = query_rot.reshape(tok_rows, kv_dev, group_size, HD)
    scores = (
        jnp.einsum("qkgd,skd->kgqs", grouped, key_rows, preferred_element_type=jnp.float32)
        * SCORE_SCALE
    )
    query_ids = jnp.arange(tok_rows)[:, None]
    key_ids = jnp.arange(key_count)[None, :]
    allowed = (key_ids > query_ids) & (key_ids <= query_ids + WINDOW)
    scores = jnp.where(allowed, scores, -jnp.inf)
    top_score = jnp.max(scores, axis=-1, keepdims=True)
    weights_soft = jnp.exp(scores - top_score)
    weights_soft = (weights_soft / jnp.sum(weights_soft, axis=-1, keepdims=True)).astype(
        jnp.bfloat16
    )
    attended = jnp.einsum(
        "kgqs,skd->qkgd", weights_soft, value_rows, preferred_element_type=jnp.float32
    )
    attended = attended.astype(jnp.bfloat16).reshape(tok_rows, heads_dev * HD)
    mixer = block_mixer()
    local_blocks = hidden.shape[1] // BLOCK
    group_index = lax.axis_index("group")
    sides = lax.axis_size("group")
    mixed = jnp.dot(
        hidden.reshape(tok_rows * local_blocks, BLOCK), mixer, preferred_element_type=jnp.float32
    )
    blocks_now = (mixed * INV_ROOT).astype(jnp.bfloat16).reshape(tok_rows, local_blocks, BLOCK)
    for section_level in range(local_blocks.bit_length() - 1):
        blocks_now = section_pairs(blocks_now, section_level)
    rotated = blocks_now.reshape(tok_rows, local_blocks * BLOCK)

    own_rows = down_codes.shape[0] // sides
    scale_rows = jnp.repeat(down_scales, GROUP, axis=0)
    codes = lax.dynamic_slice_in_dim(down_codes, group_index * own_rows, own_rows, 0)
    scales = lax.dynamic_slice_in_dim(scale_rows, group_index * own_rows, own_rows, 0)
    down_rows = (((codes - 8) * scales).astype(jnp.float32) * CODE_STEP).astype(jnp.bfloat16)
    own_out = out_weight.shape[0] // sides
    out_rows = lax.dynamic_slice_in_dim(out_weight, group_index * own_out, own_out, 0)

    half = rotated.shape[1] // sides
    rows = half // CHUNKS
    partials = jnp.dot(
        attended, gathered(out_rows), preferred_element_type=jnp.float32
    )
    for chunk in range(CHUNKS):
        piece = down_rows[chunk * rows : (chunk + 1) * rows]
        for bit_index in range(tp_count.bit_length() - 1):
            partner = swapped(piece, "tp", bit_index)
            high_side = jnp.right_shift(tp_index, bit_index) % 2
            own_values = piece.astype(jnp.float32)
            other_values = partner.astype(jnp.float32)
            piece = jnp.where(
                high_side == 0, own_values + other_values, other_values - own_values
            ).astype(jnp.bfloat16)
        left = jnp.concatenate(
            [
                rotated[:, side * half + chunk * rows : side * half + (chunk + 1) * rows]
                for side in range(sides)
            ],
            axis=1,
        )
        partials = partials + jnp.dot(left, gathered(piece), preferred_element_type=jnp.float32)
    layer_update = lax.psum_scatter(
        partials.astype(jnp.bfloat16), "tp", scatter_dimension=0, tiled=True
    )
    return layer_update


def solution(mesh):
    return jax.shard_map(
        per_device,
        mesh=mesh,
        in_specs=(
            P(("group", "seq"), "tp"),
            P(("group", "seq"), None, "tp"),
            P("group", None, "tp"),
            P("group"),
            P(("group", "seq"), "tp"),
            P("tp", "seq"),
            P("tp", "seq"),
            P("tp", "seq"),
        ),
        out_specs=P(("group", "seq", "tp"), None),
        check_vma=False,
    )
```

```python
import jax
import jax.numpy as jnp
import numpy as np
from jax import lax
from jax.sharding import PartitionSpec as P

HD = 128
WINDOW = 1024
GROUP = 128


ROPE_BASE = 10000.0
SCORE_SCALE = 168.0 ** (-0.5)
CODE_STEP = 2.0 ** (-14)
INV_ROOT = 1344.0 ** (-0.5)


def shifted(value, axis, steps):
    count = lax.axis_size(axis)
    first, last = (max(0, -steps), min(count, count - steps))
    return lax.ppermute(value, axis, [(source, source + steps) for source in range(first, last)])


def swapped(x, axis, stride):
    return lax.ppermute(x, axis, [(i, i ^ 1 << stride) for i in range(lax.axis_size(axis))])


def block_mixer():
    order = 167
    residues = {value * value % order for value in range(1, order)}
    legendre = np.array([0] + [1 if value in residues else -1 for value in range(1, order)])
    paley = np.eye(order + 1)
    paley[0, 1:] += 1
    paley[1:, 0] -= 1
    places = np.arange(order)
    paley[1:, 1:] += legendre[(places[None, :] - places[:, None]) % order]
    pair = np.array([[1, 1], [1, -1]])
    return jnp.asarray(
        np.kron(np.kron(np.kron(np.kron(pair, pair), pair), pair), paley), jnp.bfloat16
    )


def gathered(piece):
    held = {0: jnp.concatenate([piece, swapped(piece, "group", 0)], axis=0)}
    for bit_index in reversed(range(lax.axis_size("seq").bit_length() - 1)):
        for distance, columns in list(held.items()):
            held[distance | 1 << bit_index] = swapped(columns, "seq", bit_index)
    return held


def own_and_other(rows, group_index, begin, count, half):
    return jnp.concatenate(
        [
            lax.dynamic_slice_in_dim(rows, side * half + begin, count, 1)
            for side in (group_index, 1 - group_index)
        ],
        axis=1,
    )


def rotary(values, cosine, sine_part):
    half_dim = values.shape[-1] // 2
    first_half = values[..., :half_dim]
    second_half = values[..., half_dim:]
    return jnp.concatenate(
        [
            first_half * cosine - second_half * sine_part,
            second_half * cosine + first_half * sine_part,
        ],
        axis=-1,
    )


def per_device(
    queries, key_value, window_cache, span_start, hidden, down_codes, down_scales, out_weight
):
    tok_rows = queries.shape[0]
    tp_count = lax.axis_size("tp")
    seq_index = lax.axis_index("seq")
    tp_index = lax.axis_index("tp")
    heads_dev = queries.shape[1] // HD
    kv_dev = key_value.shape[2] // HD
    group_size = heads_dev // kv_dev
    first_pos = span_start[0]
    positions = first_pos + seq_index * tok_rows + jnp.arange(tok_rows, dtype=jnp.int32)
    inv_freq = ROPE_BASE ** (-(2.0 * jnp.arange(HD // 2, dtype=jnp.float32)) / HD)
    angles = positions.astype(jnp.float32)[:, None] * inv_freq[None, :]
    cosine = jnp.cos(angles)[:, None, :]
    sine_part = jnp.sin(angles)[:, None, :]
    query_rot = rotary(
        queries.reshape(tok_rows, heads_dev, HD).astype(jnp.float32), cosine, sine_part
    ).astype(jnp.bfloat16)
    key_rot = rotary(
        key_value[:, 0].reshape(tok_rows, kv_dev, HD).astype(jnp.float32), cosine, sine_part
    ).astype(jnp.bfloat16)
    own_pairs = jnp.stack([key_rot.reshape(tok_rows, kv_dev * HD), key_value[:, 1]], axis=1)
    reach_blocks = WINDOW // tok_rows
    earlier = []
    moving = own_pairs
    for hop_count in range(reach_blocks):
        moving = shifted(moving, "seq", 1)
        earlier.insert(0, moving)
    halo_rows = jnp.concatenate(earlier, axis=0)
    doubled = jnp.concatenate([window_cache, window_cache], axis=0)
    ordered = lax.dynamic_slice_in_dim(doubled, first_pos % WINDOW, WINDOW, 0)
    padded_cache = jnp.concatenate([ordered, jnp.zeros_like(ordered)], axis=0)
    from_cache = lax.dynamic_slice_in_dim(
        padded_cache, jnp.minimum(seq_index * tok_rows, WINDOW), WINDOW, 0
    )
    halo_rows = halo_rows + from_cache
    all_rows = jnp.concatenate([halo_rows, own_pairs], axis=0)
    key_count = all_rows.shape[0]
    key_rows = all_rows[:, 0].reshape(key_count, kv_dev, HD)
    value_rows = all_rows[:, 1].reshape(key_count, kv_dev, HD)
    grouped = query_rot.reshape(tok_rows, kv_dev, group_size, HD)
    scores = (
        jnp.einsum("qkgd,skd->kgqs", grouped, key_rows, preferred_element_type=jnp.float32)
        * SCORE_SCALE
    )
    query_ids = jnp.arange(tok_rows)[:, None]
    key_ids = jnp.arange(key_count)[None, :]
    allowed = (key_ids > query_ids) & (key_ids <= query_ids + WINDOW)
    scores = jnp.where(allowed, scores, -jnp.inf)
    top_score = jnp.max(scores, axis=-1, keepdims=True)
    weights_soft = jnp.exp(scores - top_score)
    weights_soft = (weights_soft / jnp.sum(weights_soft, axis=-1, keepdims=True)).astype(
        jnp.bfloat16
    )
    attended = jnp.einsum(
        "kgqs,skd->qkgd", weights_soft, value_rows, preferred_element_type=jnp.float32
    )
    attended = attended.astype(jnp.bfloat16).reshape(tok_rows, heads_dev * HD)
    group_index = lax.axis_index("group")
    mixer = block_mixer()
    width = mixer.shape[0]
    mixed = [
        jnp.dot(hidden[:, first : first + width], mixer, preferred_element_type=jnp.float32)
        for first in range(0, hidden.shape[1], width)
    ]
    stride = 1
    while stride < len(mixed):
        mixed = [
            mixed[i] + mixed[i ^ stride] if i & stride == 0 else mixed[i ^ stride] - mixed[i]
            for i in range(len(mixed))
        ]
        stride *= 2
    rotated = jnp.concatenate([(part * INV_ROOT).astype(jnp.bfloat16) for part in mixed], axis=1)

    half = rotated.shape[1] // 2
    out_half = out_weight.shape[0] // 2
    scale_rows = jnp.repeat(down_scales, GROUP, axis=0)
    unit = half // 21
    out_piece = lax.dynamic_slice_in_dim(out_weight, group_index * out_half, out_half, 0)
    tokens_left = own_and_other(attended, group_index, 0, out_half, out_half)
    totals = {
        distance: jnp.dot(tokens_left, columns, preferred_element_type=jnp.float32)
        for distance, columns in gathered(out_piece).items()
    }
    tied = None
    for first, last in ((0, 6), (6, 11), (11, 16), (16, 21)):
        begin, rows = first * unit, (last - first) * unit
        codes = lax.dynamic_slice_in_dim(down_codes, group_index * half + begin, rows, 0)
        scales = lax.dynamic_slice_in_dim(scale_rows, group_index * half + begin, rows, 0)
        piece = (((codes - 8) * scales).astype(jnp.float32) * CODE_STEP).astype(jnp.bfloat16)
        for bit_index in range(tp_count.bit_length() - 1):
            if bit_index == 0 and tied is not None:
                piece, tied = lax.optimization_barrier((piece, tied))
            partner = swapped(piece, "tp", bit_index)
            if bit_index == 0:
                tied = partner
            high_side = jnp.right_shift(tp_index, bit_index) % 2
            own_values = piece.astype(jnp.float32)
            other_values = partner.astype(jnp.float32)
            piece = jnp.where(
                high_side == 0, own_values + other_values, other_values - own_values
            ).astype(jnp.bfloat16)
        left = own_and_other(rotated, group_index, begin, rows, half)
        for distance, columns in gathered(piece).items():
            totals[distance] += jnp.dot(left, columns, preferred_element_type=jnp.float32)
    stacked = jnp.stack([totals[d].astype(jnp.bfloat16) for d in sorted(totals)])
    partials = jnp.concatenate(
        [
            lax.dynamic_index_in_dim(stacked, jnp.bitwise_xor(seq_index, s), 0, keepdims=False)
            for s in range(len(totals))
        ],
        axis=1,
    )
    return lax.psum_scatter(partials, "tp", scatter_dimension=0, tiled=True)


def solution(mesh):
    return jax.shard_map(
        per_device,
        mesh=mesh,
        in_specs=(
            P(("group", "seq"), "tp"),
            P(("group", "seq"), None, "tp"),
            P("group", None, "tp"),
            P("group"),
            P(("group", "seq"), "tp"),
            P("tp", "seq"),
            P("tp", "seq"),
            P("tp", "seq"),
        ),
        out_specs=P(("group", "seq", "tp"), None),
        check_vma=False,
    )
```

```python
import jax
import jax.numpy as jnp
import numpy as np
from jax import lax
from jax.sharding import PartitionSpec as P

HD = 128
WINDOW = 1024
GROUP = 128


ROPE_BASE = 10000.0
SCORE_SCALE = 168.0 ** (-0.5)
CODE_STEP = 2.0 ** (-14)
INV_ROOT = 1344.0 ** (-0.5)


def shifted(value, axis, steps):
    count = lax.axis_size(axis)
    first, last = (max(0, -steps), min(count, count - steps))
    return lax.ppermute(value, axis, [(source, source + steps) for source in range(first, last)])


def swapped(x, axis, stride):
    return lax.ppermute(x, axis, [(i, i ^ 1 << stride) for i in range(lax.axis_size(axis))])


def block_mixer():
    order = 167
    residues = {value * value % order for value in range(1, order)}
    legendre = np.array([0] + [1 if value in residues else -1 for value in range(1, order)])
    paley = np.eye(order + 1)
    paley[0, 1:] += 1
    paley[1:, 0] -= 1
    places = np.arange(order)
    paley[1:, 1:] += legendre[(places[None, :] - places[:, None]) % order]
    pair = np.array([[1, 1], [1, -1]])
    return jnp.asarray(
        np.kron(np.kron(np.kron(np.kron(pair, pair), pair), pair), paley), jnp.bfloat16
    )


def both_groups(piece):
    return jnp.concatenate([piece, swapped(piece, "group", 0)], axis=0)


def spread(held, bits):
    for bit_index in bits:
        for distance, columns in list(held.items()):
            held[distance | 1 << bit_index] = swapped(columns, "seq", bit_index)
    return held


def over_chips(piece, seq_first):
    bits = list(reversed(range(1, lax.axis_size("seq").bit_length() - 1)))
    if seq_first:
        return {d: both_groups(part) for d, part in spread({0: piece}, bits).items()}
    return spread({0: both_groups(piece)}, bits)


def own_and_other(rows, group_index, begin, count, half):
    return jnp.concatenate(
        [
            lax.dynamic_slice_in_dim(rows, side * half + begin, count, 1)
            for side in (group_index, 1 - group_index)
        ],
        axis=1,
    )


def rotary(values, cosine, sine_part):
    half_dim = values.shape[-1] // 2
    first_half = values[..., :half_dim]
    second_half = values[..., half_dim:]
    return jnp.concatenate(
        [
            first_half * cosine - second_half * sine_part,
            second_half * cosine + first_half * sine_part,
        ],
        axis=-1,
    )


def per_device(
    queries, key_value, window_cache, span_start, hidden, down_codes, down_scales, out_weight
):
    tok_rows = queries.shape[0]
    tp_count = lax.axis_size("tp")
    seq_index = lax.axis_index("seq")
    tp_index = lax.axis_index("tp")
    heads_dev = queries.shape[1] // HD
    kv_dev = key_value.shape[2] // HD
    group_size = heads_dev // kv_dev
    first_pos = span_start[0]
    positions = first_pos + seq_index * tok_rows + jnp.arange(tok_rows, dtype=jnp.int32)
    inv_freq = ROPE_BASE ** (-(2.0 * jnp.arange(HD // 2, dtype=jnp.float32)) / HD)
    angles = positions.astype(jnp.float32)[:, None] * inv_freq[None, :]
    cosine = jnp.cos(angles)[:, None, :]
    sine_part = jnp.sin(angles)[:, None, :]
    query_rot = rotary(
        queries.reshape(tok_rows, heads_dev, HD).astype(jnp.float32), cosine, sine_part
    ).astype(jnp.bfloat16)
    key_rot = rotary(
        key_value[:, 0].reshape(tok_rows, kv_dev, HD).astype(jnp.float32), cosine, sine_part
    ).astype(jnp.bfloat16)
    own_pairs = jnp.stack([key_rot.reshape(tok_rows, kv_dev * HD), key_value[:, 1]], axis=1)
    reach_blocks = WINDOW // tok_rows
    earlier = []
    moving = own_pairs
    for hop_count in range(reach_blocks):
        moving = shifted(moving, "seq", 1)
        earlier.insert(0, moving)
    halo_rows = jnp.concatenate(earlier, axis=0)
    doubled = jnp.concatenate([window_cache, window_cache], axis=0)
    ordered = lax.dynamic_slice_in_dim(doubled, first_pos % WINDOW, WINDOW, 0)
    padded_cache = jnp.concatenate([ordered, jnp.zeros_like(ordered)], axis=0)
    from_cache = lax.dynamic_slice_in_dim(
        padded_cache, jnp.minimum(seq_index * tok_rows, WINDOW), WINDOW, 0
    )
    halo_rows = halo_rows + from_cache
    all_rows = jnp.concatenate([halo_rows, own_pairs], axis=0)
    key_count = all_rows.shape[0]
    key_rows = all_rows[:, 0].reshape(key_count, kv_dev, HD)
    value_rows = all_rows[:, 1].reshape(key_count, kv_dev, HD)
    grouped = query_rot.reshape(tok_rows, kv_dev, group_size, HD)
    scores = (
        jnp.einsum("qkgd,skd->kgqs", grouped, key_rows, preferred_element_type=jnp.float32)
        * SCORE_SCALE
    )
    query_ids = jnp.arange(tok_rows)[:, None]
    key_ids = jnp.arange(key_count)[None, :]
    allowed = (key_ids > query_ids) & (key_ids <= query_ids + WINDOW)
    scores = jnp.where(allowed, scores, -jnp.inf)
    top_score = jnp.max(scores, axis=-1, keepdims=True)
    weights_soft = jnp.exp(scores - top_score)
    weights_soft = (weights_soft / jnp.sum(weights_soft, axis=-1, keepdims=True)).astype(
        jnp.bfloat16
    )
    attended = jnp.einsum(
        "kgqs,skd->qkgd", weights_soft, value_rows, preferred_element_type=jnp.float32
    )
    attended = attended.astype(jnp.bfloat16).reshape(tok_rows, heads_dev * HD)
    group_index = lax.axis_index("group")
    mixer = block_mixer()
    width = mixer.shape[0]
    mixed = [
        jnp.dot(hidden[:, first : first + width], mixer, preferred_element_type=jnp.float32)
        for first in range(0, hidden.shape[1], width)
    ]
    stride = 1
    while stride < len(mixed):
        mixed = [
            mixed[i] + mixed[i ^ stride] if i & stride == 0 else mixed[i ^ stride] - mixed[i]
            for i in range(len(mixed))
        ]
        stride *= 2
    rotated = jnp.concatenate([(part * INV_ROOT).astype(jnp.bfloat16) for part in mixed], axis=1)

    half = rotated.shape[1] // 2
    out_half = out_weight.shape[0] // 2
    unit = half // 21
    out_piece = lax.dynamic_slice_in_dim(out_weight, group_index * out_half, out_half, 0)
    tokens_left = own_and_other(attended, group_index, 0, out_half, out_half)
    out_wide = over_chips(out_piece, True)
    wides = []
    lefts = []
    tied = None
    for chunk, (first, last) in enumerate(((0, 6), (6, 12), (12, 17), (17, 21))):
        begin, rows = first * unit, (last - first) * unit
        codes = lax.dynamic_slice_in_dim(down_codes, group_index * half + begin, rows, 0)
        if unit % GROUP == 0:
            scales = lax.dynamic_slice_in_dim(
                down_scales, (group_index * half + begin) // GROUP, rows // GROUP, 0
            )
            codes = codes.reshape(rows // GROUP, GROUP, codes.shape[1])
            scales = scales[:, None, :]
        else:
            scale_rows = jnp.repeat(down_scales, GROUP, axis=0)
            scales = lax.dynamic_slice_in_dim(scale_rows, group_index * half + begin, rows, 0)
        piece = (((codes - 8) * scales).astype(jnp.float32) * CODE_STEP).astype(jnp.bfloat16)
        piece = piece.reshape(rows, piece.shape[-1])
        for bit_index in range(tp_count.bit_length() - 1):
            if bit_index == 0 and tied is not None:
                piece, tied = lax.optimization_barrier((piece, tied))
            if bit_index == 1 and chunk == 1:
                piece, out_wide = lax.optimization_barrier((piece, out_wide))
            if bit_index == 1 and chunk == 3:
                piece, wides[0] = lax.optimization_barrier((piece, wides[0]))
            partner = swapped(piece, "tp", bit_index)
            if bit_index == 0:
                tied = partner
            high_side = jnp.right_shift(tp_index, bit_index) % 2
            own_values = piece.astype(jnp.float32)
            other_values = partner.astype(jnp.float32)
            piece = jnp.where(
                high_side == 0, own_values + other_values, other_values - own_values
            ).astype(jnp.bfloat16)
        lefts.append(own_and_other(rotated, group_index, begin, rows, half))
        wides.append(over_chips(piece, chunk < 2))
    totals = {
        distance: jnp.dot(tokens_left, columns, preferred_element_type=jnp.float32)
        for distance, columns in spread(out_wide, [0]).items()
    }
    for left, wide in zip(lefts, wides):
        for distance, columns in spread(wide, [0]).items():
            totals[distance] += jnp.dot(left, columns, preferred_element_type=jnp.float32)
    stacked = jnp.stack([totals[d].astype(jnp.bfloat16) for d in sorted(totals)])
    partials = jnp.concatenate(
        [
            lax.dynamic_index_in_dim(stacked, jnp.bitwise_xor(seq_index, s), 0, keepdims=False)
            for s in range(len(totals))
        ],
        axis=1,
    )
    return lax.psum_scatter(partials, "tp", scatter_dimension=0, tiled=True)


def solution(mesh):
    return jax.shard_map(
        per_device,
        mesh=mesh,
        in_specs=(
            P(("group", "seq"), "tp"),
            P(("group", "seq"), None, "tp"),
            P("group", None, "tp"),
            P("group"),
            P(("group", "seq"), "tp"),
            P("tp", "seq"),
            P("tp", "seq"),
            P("tp", "seq"),
        ),
        out_specs=P(("group", "seq", "tp"), None),
        check_vma=False,
    )
```

```python
import jax
import jax.numpy as jnp
import numpy as np
from jax import lax
from jax.sharding import PartitionSpec as P

HD = 128
WINDOW = 1024
GROUP = 128


ROPE_BASE = 10000.0
SCORE_SCALE = 168.0 ** (-0.5)
CODE_STEP = 2.0 ** (-14)
INV_ROOT = 1344.0 ** (-0.5)


def shifted(value, axis, steps):
    count = lax.axis_size(axis)
    first, last = (max(0, -steps), min(count, count - steps))
    return lax.ppermute(value, axis, [(source, source + steps) for source in range(first, last)])


def swapped(x, axis, stride):
    return lax.ppermute(x, axis, [(i, i ^ 1 << stride) for i in range(lax.axis_size(axis))])


def block_mixer():
    order = 167
    residues = {value * value % order for value in range(1, order)}
    legendre = np.array([0] + [1 if value in residues else -1 for value in range(1, order)])
    paley = np.eye(order + 1)
    paley[0, 1:] += 1
    paley[1:, 0] -= 1
    places = np.arange(order)
    paley[1:, 1:] += legendre[(places[None, :] - places[:, None]) % order]
    pair = np.array([[1, 1], [1, -1]])
    return jnp.asarray(
        np.kron(np.kron(np.kron(np.kron(pair, pair), pair), pair), paley), jnp.bfloat16
    )


def both_groups(piece):
    return jnp.concatenate([piece, swapped(piece, "group", 0)], axis=0)


def spread(held, bits):
    for bit_index in bits:
        for distance, columns in list(held.items()):
            held[distance | 1 << bit_index] = swapped(columns, "seq", bit_index)
    return held


def over_chips(piece, seq_first):
    bits = list(reversed(range(1, lax.axis_size("seq").bit_length() - 1)))
    if seq_first:
        return {d: both_groups(part) for d, part in spread({0: piece}, bits).items()}
    return spread({0: both_groups(piece)}, bits)


def own_and_other(rows, group_index, begin, count, half):
    return jnp.concatenate(
        [
            lax.dynamic_slice_in_dim(rows, side * half + begin, count, 1)
            for side in (group_index, 1 - group_index)
        ],
        axis=1,
    )


def rotary(values, cosine, sine_part):
    half_dim = values.shape[-1] // 2
    first_half = values[..., :half_dim]
    second_half = values[..., half_dim:]
    return jnp.concatenate(
        [
            first_half * cosine - second_half * sine_part,
            second_half * cosine + first_half * sine_part,
        ],
        axis=-1,
    )


def per_device(
    queries, key_value, window_cache, span_start, hidden, down_codes, down_scales, out_weight
):
    tok_rows = queries.shape[0]
    tp_count = lax.axis_size("tp")
    seq_index = lax.axis_index("seq")
    tp_index = lax.axis_index("tp")
    heads_dev = queries.shape[1] // HD
    kv_dev = key_value.shape[2] // HD
    group_size = heads_dev // kv_dev
    first_pos = span_start[0]
    positions = first_pos + seq_index * tok_rows + jnp.arange(tok_rows, dtype=jnp.int32)
    inv_freq = ROPE_BASE ** (-(2.0 * jnp.arange(HD // 2, dtype=jnp.float32)) / HD)
    angles = positions.astype(jnp.float32)[:, None] * inv_freq[None, :]
    cosine = jnp.cos(angles)[:, None, :]
    sine_part = jnp.sin(angles)[:, None, :]
    query_rot = rotary(
        queries.reshape(tok_rows, heads_dev, HD).astype(jnp.float32), cosine, sine_part
    ).astype(jnp.bfloat16)
    key_rot = rotary(
        key_value[:, 0].reshape(tok_rows, kv_dev, HD).astype(jnp.float32), cosine, sine_part
    ).astype(jnp.bfloat16)
    own_pairs = jnp.stack([key_rot.reshape(tok_rows, kv_dev * HD), key_value[:, 1]], axis=1)
    reach_blocks = WINDOW // tok_rows
    earlier = []
    moving = own_pairs
    for hop_count in range(reach_blocks):
        moving = shifted(moving, "seq", 1)
        earlier.insert(0, moving)
    halo_rows = jnp.concatenate(earlier, axis=0)
    doubled = jnp.concatenate([window_cache, window_cache], axis=0)
    ordered = lax.dynamic_slice_in_dim(doubled, first_pos % WINDOW, WINDOW, 0)
    padded_cache = jnp.concatenate([ordered, jnp.zeros_like(ordered)], axis=0)
    from_cache = lax.dynamic_slice_in_dim(
        padded_cache, jnp.minimum(seq_index * tok_rows, WINDOW), WINDOW, 0
    )
    halo_rows = halo_rows + from_cache
    all_rows = jnp.concatenate([halo_rows, own_pairs], axis=0)
    key_count = all_rows.shape[0]
    key_rows = all_rows[:, 0].reshape(key_count, kv_dev, HD)
    value_rows = all_rows[:, 1].reshape(key_count, kv_dev, HD)
    grouped = query_rot.reshape(tok_rows, kv_dev, group_size, HD)
    scores = (
        jnp.einsum("qkgd,skd->kgqs", grouped, key_rows, preferred_element_type=jnp.float32)
        * SCORE_SCALE
    )
    query_ids = jnp.arange(tok_rows)[:, None]
    key_ids = jnp.arange(key_count)[None, :]
    allowed = (key_ids > query_ids) & (key_ids <= query_ids + WINDOW)
    scores = jnp.where(allowed, scores, -jnp.inf)
    top_score = jnp.max(scores, axis=-1, keepdims=True)
    weights_soft = jnp.exp(scores - top_score)
    weights_soft = (weights_soft / jnp.sum(weights_soft, axis=-1, keepdims=True)).astype(
        jnp.bfloat16
    )
    attended = jnp.einsum(
        "kgqs,skd->qkgd", weights_soft, value_rows, preferred_element_type=jnp.float32
    )
    attended = attended.astype(jnp.bfloat16).reshape(tok_rows, heads_dev * HD)
    group_index = lax.axis_index("group")
    mixer = block_mixer()
    width = mixer.shape[0]
    mixed = [
        jnp.dot(hidden[:, first : first + width], mixer, preferred_element_type=jnp.float32)
        for first in range(0, hidden.shape[1], width)
    ]
    stride = 1
    while stride < len(mixed):
        mixed = [
            mixed[i] + mixed[i ^ stride] if i & stride == 0 else mixed[i ^ stride] - mixed[i]
            for i in range(len(mixed))
        ]
        stride *= 2
    rotated = jnp.concatenate([(part * INV_ROOT).astype(jnp.bfloat16) for part in mixed], axis=1)

    half = rotated.shape[1] // 2
    out_half = out_weight.shape[0] // 2
    unit = half // 21
    out_piece = lax.dynamic_slice_in_dim(out_weight, group_index * out_half, out_half, 0)
    tokens_left = own_and_other(attended, group_index, 0, out_half, out_half)
    out_wide = over_chips(out_piece, True)
    wides = []
    lefts = []
    tied = None
    for chunk, (first, last) in enumerate(((0, 6), (6, 12), (12, 17), (17, 21))):
        begin, rows = first * unit, (last - first) * unit
        codes = lax.dynamic_slice_in_dim(down_codes, group_index * half + begin, rows, 0)
        if unit % GROUP == 0:
            scales = lax.dynamic_slice_in_dim(
                down_scales, (group_index * half + begin) // GROUP, rows // GROUP, 0
            )
            codes = codes.reshape(rows // GROUP, GROUP, codes.shape[1])
            scales = scales[:, None, :]
        else:
            scale_rows = jnp.repeat(down_scales, GROUP, axis=0)
            scales = lax.dynamic_slice_in_dim(scale_rows, group_index * half + begin, rows, 0)
        piece = (((codes - 8) * scales).astype(jnp.float32) * CODE_STEP).astype(jnp.bfloat16)
        piece = piece.reshape(rows, piece.shape[-1])
        for bit_index in range(tp_count.bit_length() - 1):
            if bit_index == 0 and tied is not None:
                piece, tied = lax.optimization_barrier((piece, tied))
            if bit_index == 1 and chunk == 1:
                piece, out_wide = lax.optimization_barrier((piece, out_wide))
            if bit_index == 1 and chunk == 3:
                piece, wides[0] = lax.optimization_barrier((piece, wides[0]))
            partner = swapped(piece, "tp", bit_index)
            if bit_index == 0:
                tied = partner
            high_side = jnp.right_shift(tp_index, bit_index) % 2
            own_values = piece.astype(jnp.float32)
            other_values = partner.astype(jnp.float32)
            piece = jnp.where(
                high_side == 0, own_values + other_values, other_values - own_values
            ).astype(jnp.bfloat16)
        lefts.append(own_and_other(rotated, group_index, begin, rows, half))
        wides.append(over_chips(piece, True))
    totals = {
        distance: jnp.dot(tokens_left, columns, preferred_element_type=jnp.float32)
        for distance, columns in spread(out_wide, [0]).items()
    }
    for left, wide in zip(lefts, wides):
        for distance, columns in spread(wide, [0]).items():
            totals[distance] += jnp.dot(left, columns, preferred_element_type=jnp.float32)
    stacked = jnp.stack([totals[d].astype(jnp.bfloat16) for d in sorted(totals)])
    partials = jnp.concatenate(
        [
            lax.dynamic_index_in_dim(stacked, jnp.bitwise_xor(seq_index, s), 0, keepdims=False)
            for s in range(len(totals))
        ],
        axis=1,
    )
    return lax.psum_scatter(partials, "tp", scatter_dimension=0, tiled=True)


def solution(mesh):
    return jax.shard_map(
        per_device,
        mesh=mesh,
        in_specs=(
            P(("group", "seq"), "tp"),
            P(("group", "seq"), None, "tp"),
            P("group", None, "tp"),
            P("group"),
            P(("group", "seq"), "tp"),
            P("tp", "seq"),
            P("tp", "seq"),
            P("tp", "seq"),
        ),
        out_specs=P(("group", "seq", "tp"), None),
        check_vma=False,
    )
```

```python
import jax
import jax.numpy as jnp
import numpy as np
from jax import lax
from jax.sharding import PartitionSpec as P

HD = 128
WINDOW = 1024
GROUP = 128


ROPE_BASE = 10000.0
SCORE_SCALE = 168.0 ** (-0.5)
CODE_STEP = 2.0 ** (-14)
INV_ROOT = 1344.0 ** (-0.5)


def shifted(value, axis, steps):
    count = lax.axis_size(axis)
    first, last = (max(0, -steps), min(count, count - steps))
    return lax.ppermute(value, axis, [(source, source + steps) for source in range(first, last)])


def swapped(x, axis, stride):
    return lax.ppermute(x, axis, [(i, i ^ 1 << stride) for i in range(lax.axis_size(axis))])


def block_mixer():
    order = 167
    residues = {value * value % order for value in range(1, order)}
    legendre = np.array([0] + [1 if value in residues else -1 for value in range(1, order)])
    paley = np.eye(order + 1)
    paley[0, 1:] += 1
    paley[1:, 0] -= 1
    places = np.arange(order)
    paley[1:, 1:] += legendre[(places[None, :] - places[:, None]) % order]
    pair = np.array([[1, 1], [1, -1]])
    return jnp.asarray(
        np.kron(np.kron(np.kron(np.kron(pair, pair), pair), pair), paley), jnp.bfloat16
    )


def both_groups(piece):
    return jnp.concatenate([piece, swapped(piece, "group", 0)], axis=0)


def spread(held, bits):
    for bit_index in bits:
        for distance, columns in list(held.items()):
            held[distance | 1 << bit_index] = swapped(columns, "seq", bit_index)
    return held


def over_chips(piece, seq_first):
    bits = list(reversed(range(1, lax.axis_size("seq").bit_length() - 1)))
    if seq_first:
        return {d: both_groups(part) for d, part in spread({0: piece}, bits).items()}
    return spread({0: both_groups(piece)}, bits)


def own_and_other(rows, group_index, begin, count, half):
    return jnp.concatenate(
        [
            lax.dynamic_slice_in_dim(rows, side * half + begin, count, 1)
            for side in (group_index, 1 - group_index)
        ],
        axis=1,
    )


def rotary(values, cosine, sine_part):
    half_dim = values.shape[-1] // 2
    first_half = values[..., :half_dim]
    second_half = values[..., half_dim:]
    return jnp.concatenate(
        [
            first_half * cosine - second_half * sine_part,
            second_half * cosine + first_half * sine_part,
        ],
        axis=-1,
    )


def per_device(
    queries, key_value, window_cache, span_start, hidden, down_codes, down_scales, out_weight
):
    tok_rows = queries.shape[0]
    tp_count = lax.axis_size("tp")
    seq_index = lax.axis_index("seq")
    tp_index = lax.axis_index("tp")
    heads_dev = queries.shape[1] // HD
    kv_dev = key_value.shape[2] // HD
    group_size = heads_dev // kv_dev
    first_pos = span_start[0]
    positions = first_pos + seq_index * tok_rows + jnp.arange(tok_rows, dtype=jnp.int32)
    inv_freq = ROPE_BASE ** (-(2.0 * jnp.arange(HD // 2, dtype=jnp.float32)) / HD)
    angles = positions.astype(jnp.float32)[:, None] * inv_freq[None, :]
    cosine = jnp.cos(angles)[:, None, :]
    sine_part = jnp.sin(angles)[:, None, :]
    query_rot = rotary(
        queries.reshape(tok_rows, heads_dev, HD).astype(jnp.float32), cosine, sine_part
    ).astype(jnp.bfloat16)
    key_rot = rotary(
        key_value[:, 0].reshape(tok_rows, kv_dev, HD).astype(jnp.float32), cosine, sine_part
    ).astype(jnp.bfloat16)
    own_pairs = jnp.stack([key_rot.reshape(tok_rows, kv_dev * HD), key_value[:, 1]], axis=1)
    reach_blocks = WINDOW // tok_rows
    earlier = []
    moving = own_pairs
    for hop_count in range(reach_blocks):
        moving = shifted(moving, "seq", 1)
        earlier.insert(0, moving)
    halo_rows = jnp.concatenate(earlier, axis=0)
    doubled = jnp.concatenate([window_cache, window_cache], axis=0)
    ordered = lax.dynamic_slice_in_dim(doubled, first_pos % WINDOW, WINDOW, 0)
    padded_cache = jnp.concatenate([ordered, jnp.zeros_like(ordered)], axis=0)
    from_cache = lax.dynamic_slice_in_dim(
        padded_cache, jnp.minimum(seq_index * tok_rows, WINDOW), WINDOW, 0
    )
    halo_rows = halo_rows + from_cache
    all_rows = jnp.concatenate([halo_rows, own_pairs], axis=0)
    key_count = all_rows.shape[0]
    key_rows = all_rows[:, 0].reshape(key_count, kv_dev, HD)
    value_rows = all_rows[:, 1].reshape(key_count, kv_dev, HD)
    grouped = query_rot.reshape(tok_rows, kv_dev, group_size, HD)
    scores = (
        jnp.einsum("qkgd,skd->kgqs", grouped, key_rows, preferred_element_type=jnp.float32)
        * SCORE_SCALE
    )
    query_ids = jnp.arange(tok_rows)[:, None]
    key_ids = jnp.arange(key_count)[None, :]
    allowed = (key_ids > query_ids) & (key_ids <= query_ids + WINDOW)
    scores = jnp.where(allowed, scores, -jnp.inf)
    top_score = jnp.max(scores, axis=-1, keepdims=True)
    weights_soft = jnp.exp(scores - top_score)
    weights_soft = (weights_soft / jnp.sum(weights_soft, axis=-1, keepdims=True)).astype(
        jnp.bfloat16
    )
    attended = jnp.einsum(
        "kgqs,skd->qkgd", weights_soft, value_rows, preferred_element_type=jnp.float32
    )
    attended = attended.astype(jnp.bfloat16).reshape(tok_rows, heads_dev * HD)
    group_index = lax.axis_index("group")
    mixer = block_mixer()
    width = mixer.shape[0]
    mixed = [
        jnp.dot(hidden[:, first : first + width], mixer, preferred_element_type=jnp.float32)
        for first in range(0, hidden.shape[1], width)
    ]
    stride = 1
    while stride < len(mixed):
        mixed = [
            mixed[i] + mixed[i ^ stride] if i & stride == 0 else mixed[i ^ stride] - mixed[i]
            for i in range(len(mixed))
        ]
        stride *= 2
    rotated = jnp.concatenate([(part * INV_ROOT).astype(jnp.bfloat16) for part in mixed], axis=1)

    half = rotated.shape[1] // 2
    out_half = out_weight.shape[0] // 2
    unit = half // 21
    out_piece = lax.dynamic_slice_in_dim(out_weight, group_index * out_half, out_half, 0)
    tokens_left = own_and_other(attended, group_index, 0, out_half, out_half)
    out_wide = over_chips(out_piece, True)
    wides = []
    lefts = []
    tied = None
    for chunk, (first, last) in enumerate(((0, 5), (5, 12), (12, 18), (18, 21))):
        begin, rows = first * unit, (last - first) * unit
        codes = lax.dynamic_slice_in_dim(down_codes, group_index * half + begin, rows, 0)
        if unit % GROUP == 0:
            scales = lax.dynamic_slice_in_dim(
                down_scales, (group_index * half + begin) // GROUP, rows // GROUP, 0
            )
            codes = codes.reshape(rows // GROUP, GROUP, codes.shape[1])
            scales = scales[:, None, :]
        else:
            scale_rows = jnp.repeat(down_scales, GROUP, axis=0)
            scales = lax.dynamic_slice_in_dim(scale_rows, group_index * half + begin, rows, 0)
        piece = (((codes - 8) * scales).astype(jnp.float32) * CODE_STEP).astype(jnp.bfloat16)
        piece = piece.reshape(rows, piece.shape[-1])
        for bit_index in range(tp_count.bit_length() - 1):
            if bit_index == 0 and tied is not None:
                piece, tied = lax.optimization_barrier((piece, tied))
            if bit_index == 1 and chunk == 1:
                piece, out_wide = lax.optimization_barrier((piece, out_wide))
            if bit_index == 1 and chunk == 3:
                piece, wides[0] = lax.optimization_barrier((piece, wides[0]))
            partner = swapped(piece, "tp", bit_index)
            if bit_index == 0:
                tied = partner
            high_side = jnp.right_shift(tp_index, bit_index) % 2
            own_values = piece.astype(jnp.float32)
            other_values = partner.astype(jnp.float32)
            piece = jnp.where(
                high_side == 0, own_values + other_values, other_values - own_values
            ).astype(jnp.bfloat16)
        lefts.append(own_and_other(rotated, group_index, begin, rows, half))
        wides.append(over_chips(piece, True))
    totals = {
        distance: jnp.dot(tokens_left, columns, preferred_element_type=jnp.float32)
        for distance, columns in spread(out_wide, [0]).items()
    }
    for left, wide in zip(lefts, wides):
        for distance, columns in spread(wide, [0]).items():
            totals[distance] += jnp.dot(left, columns, preferred_element_type=jnp.float32)
    stacked = jnp.stack([totals[d].astype(jnp.bfloat16) for d in sorted(totals)])
    partials = jnp.concatenate(
        [
            lax.dynamic_index_in_dim(stacked, jnp.bitwise_xor(seq_index, s), 0, keepdims=False)
            for s in range(len(totals))
        ],
        axis=1,
    )
    return lax.psum_scatter(partials, "tp", scatter_dimension=0, tiled=True)


def solution(mesh):
    return jax.shard_map(
        per_device,
        mesh=mesh,
        in_specs=(
            P(("group", "seq"), "tp"),
            P(("group", "seq"), None, "tp"),
            P("group", None, "tp"),
            P("group"),
            P(("group", "seq"), "tp"),
            P("tp", "seq"),
            P("tp", "seq"),
            P("tp", "seq"),
        ),
        out_specs=P(("group", "seq", "tp"), None),
        check_vma=False,
    )
```
